32 devices in a mesh: groups: 2 (over y), expert: 16 (over z, x, core), sub: 1.
Axes of the slice: x: 2, y: 2, z: 4, core: 2. Of those that a mesh axis runs over, the one named last changes fastest.
Arguments:
- tokens: bfloat16 [2048, 2048], P(('groups', 'expert', 'sub')), parts along dimension 0, may hold values from -6 to 6
- router_probs: float32 [2048, 8], P(('groups', 'expert', 'sub')), parts along dimension 0, may hold values from 0.05 to 1
- expert_ids: int32 [2048, 8], P(('groups', 'expert', 'sub')), parts along dimension 0, may hold values from 0 to 15, all different within a row; in each aligned block of 64 rows (0 to 63, 64 to 127, ...) at most 32 rows name the same one
- slot_expert: int32 [16], replicated, may hold values from 0 to 15, each once
- w_gate: bfloat16 [16, 2048, 768], P('expert', None, 'sub'), may hold values from -0.125 to 0.125
- w_up: bfloat16 [16, 2048, 768], P('expert', None, 'sub'), may hold values from -0.125 to 0.125
- w_down: bfloat16 [16, 768, 2048], P('expert', 'sub'), may hold values from -0.21875 to 0.21875
Outputs:
- mixed: bfloat16 [2048, 2048], P(('groups', 'expert', 'sub')), parts along dimension 0
The draws below stay inside these ranges and needn't reach their ends.
There are 2 independent parts, one for each index of `groups`. The reference program is written for one: setup_inputs(seed, part) draws one part's arguments, and reference() takes and returns one part's arrays. A program takes and returns all parts, laid end to end along the dimension named above; an argument that names none is the same for every part. Nothing has to cross between parts.
Inputs may be any that keep to these rules, and one draw needn't show every extreme that they name: `expert_ids`: each row names 8 different experts. Among the rows of one device (aligned blocks of 64 rows) no expert is named more than 32 times, a bound that some block reaches. `slot_expert`: each expert stands in exactly one slot.
All inputs are finite; a program needn't handle non-finite values.
Results may differ from the reference program's by a relative error of at most 0.013.
Values may be sent and summed in bfloat16 or wider, within the bound.
A program may use at most 64 MiB of HBM per device.

```python
import math
import jax
import jax.numpy as jnp
import numpy as np
from jax import lax

D = 2048
FF = 768
TOP = 8
TOK_DEV = 64
EXPERTS = 16
CAP = 32
TOKENS = 1024
N_EXPERT = 16
N_SUB = 1


def block_levels(stream_key, shape, shards, least, high):
    loudness = 1.0
    for axis_at, blocks in shards:
        heights = jax.random.uniform(jax.random.fold_in(jax.random.fold_in(stream_key, 6), axis_at), (blocks,), jnp.float32, least / len(shards), high / len(shards))
        loudness = loudness * jnp.repeat(jnp.exp(heights), shape[axis_at] // blocks).reshape((-1,) + (1,) * (len(shape) - 1 - axis_at))
    return loudness


def shared_out(key, own, number, rows, amount, top, most, lean):
    order = jax.random.permutation(key, amount)
    heavy_load, usual = load_shares(amount, rows * top, most, lean, True), load_shares(amount, rows * top, most, lean, False)
    places = jnp.arange(amount)

    def named(sizes, turn):
        used = int((sizes > 0).sum())
        fixed = max(1, used // 4)
        passed = fixed + (places - fixed + turn * (used - fixed)) % max(1, amount - fixed)
        return jnp.zeros((amount,), jnp.int32).at[order[jnp.where(places < fixed, places, passed)]].set(jnp.asarray(sizes, jnp.int32))

    sizes = jnp.where(number % 4 == 0, named(heavy_load, number // 4), named(usual, number - number // 4 - 1))
    mixed = jax.random.permutation(jax.random.fold_in(own, 3), amount)
    giver, taker = mixed[0:amount // 2 * 2:2], mixed[1:amount // 2 * 2:2]
    margin = jnp.minimum(sizes[giver] - 1, most - sizes[taker]) // 2
    margin = jnp.where((giver == order[0]) | (taker == order[0]) | (sizes[taker] == 0), 0, jnp.maximum(margin, 0))
    passed = jax.random.randint(jax.random.fold_in(own, 4), (amount // 2,), 0, 1 << 20) % (margin + 1)
    sizes = sizes.at[giver].add(-passed).at[taker].add(passed)
    items = jnp.searchsorted(jnp.cumsum(sizes), jnp.arange(rows * top), side="right").astype(jnp.int32)
    table = items.reshape(top, rows).T
    table = table[jax.random.permutation(jax.random.fold_in(own, 1), rows)]
    turn = jax.random.randint(jax.random.fold_in(own, 2), (rows, 1), 0, top)
    return jnp.take_along_axis(table, (jnp.arange(top)[None, :] + turn) % top, axis=1)


def load_shares(number_of, total, limit, lean, full):
    loads = [(1 << 20) // math.isqrt(rank ** lean) + 1 for rank in range(1, number_of + 1)]
    largest = limit if full else min(limit, max(-(-total // number_of), total * loads[0] // sum(loads)))
    least = 1 if total - largest >= number_of - 1 else 0
    holding, surplus = [largest] + [least] * (number_of - 1), total - largest - least * (number_of - 1)
    while surplus > 0:
        candidates = [i for i in range(1, number_of) if holding[i] < largest] or [i for i in range(1, number_of) if holding[i] < limit]
        pool, remaining = sum([loads[i] for i in candidates]), surplus
        for i in candidates:
            extra = min(limit - holding[i], max(1, remaining * loads[i] // pool), surplus)
            holding[i] = holding[i] + extra
            surplus = surplus - extra
    return np.array(holding)


def normal_values(stream_key, extent, deviation, most, shards=(), held_as=jnp.bfloat16):
    loudness = block_levels(stream_key, extent, shards, -0.22, 0.18) if shards else 1.0
    result = jax.random.normal(stream_key, extent, jnp.float32) * deviation * loudness
    return jnp.minimum(jnp.maximum(result, -most), most).astype(held_as)


def setup_inputs(seed: int = 0, part: int = 0) -> dict:
    streams_of = jax.random.split(jax.random.key(seed), 8)
    part_keys = jax.random.split(jax.random.fold_in(streams_of[7], part), 8)
    tokens = normal_values(part_keys[0], (TOKENS, D), 1.0, 6.0, ((0, 16),))
    router_probs = jnp.clip(0.05 + 0.95 * jax.random.uniform(part_keys[1], (TOKENS, TOP), jnp.float32) ** block_levels(part_keys[1], (TOKENS, TOP), ((0, 16),), -0.2, 0.2), 0.05, 1.0)
    expert_ids_keys = jax.random.split(jax.random.fold_in(part_keys[2], 1), TOKENS // TOK_DEV)
    expert_ids_turns = jax.random.permutation(jax.random.fold_in(part_keys[2], 3), TOKENS // TOK_DEV)
    expert_ids = jax.vmap(lambda own, number: shared_out(jax.random.fold_in(part_keys[2], 2), own, number, TOK_DEV, EXPERTS, TOP, CAP, 0))(expert_ids_keys, expert_ids_turns).reshape((TOKENS, TOP))
    slot_expert = jax.random.permutation(streams_of[3], EXPERTS).astype(jnp.int32)
    w_gate = normal_values(streams_of[4], (EXPERTS, D, FF), D ** -0.5, 0.125, ((0, 16),))
    w_up = normal_values(streams_of[5], (EXPERTS, D, FF), D ** -0.5, 0.125, ((0, 16),))
    w_down = normal_values(streams_of[6], (EXPERTS, FF, D), FF ** -0.5, 0.21875, ((0, 16),))
    return {"tokens": tokens, "router_probs": router_probs, "expert_ids": expert_ids, "slot_expert": slot_expert, "w_gate": w_gate, "w_up": w_up, "w_down": w_down}


def reference(tokens, router_probs, expert_ids, slot_expert, w_gate, w_up, w_down):
    gates = router_probs / jnp.sum(router_probs, axis=1, keepdims=True)
    block = FF // N_SUB
    bound = N_EXPERT * N_SUB * CAP

    def one_slot(mixed, slot):
        expert = slot_expert[slot]
        picked = expert_ids == expert
        weight = jnp.sum(jnp.where(picked, gates, jnp.float32(0.0)), axis=1)
        routed = jnp.any(picked, axis=1)
        index = jnp.nonzero(routed, size=bound, fill_value=TOKENS)[0].astype(jnp.int32)
        rows = jnp.take(tokens, index, axis=0, mode="fill", fill_value=0)
        scale = jnp.take(weight, index, axis=0, mode="fill", fill_value=0)
        gate_in = jnp.dot(rows, w_gate[slot], preferred_element_type=jnp.float32)
        up_in = jnp.dot(rows, w_up[slot], preferred_element_type=jnp.float32)
        hidden = (jax.nn.silu(gate_in) * up_in).astype(jnp.bfloat16)
        total = jnp.zeros((bound, D), jnp.float32)
        for part in range(N_SUB):
            piece = jnp.dot(hidden[:, part * block:(part + 1) * block], w_down[slot, part * block:(part + 1) * block], preferred_element_type=jnp.float32).astype(jnp.bfloat16)
            piece = lax.optimization_barrier(piece)
            total = total + piece.astype(jnp.float32)
        output = lax.optimization_barrier(total.astype(jnp.bfloat16))
        mixed = mixed.at[index].add(scale[:, None] * output.astype(jnp.float32), mode="drop")
        return mixed, None

    start = jnp.zeros((TOKENS, D), jnp.float32)
    mixed, unused = lax.scan(one_slot, start, jnp.arange(EXPERTS, dtype=jnp.int32))
    return mixed.astype(jnp.bfloat16)
```

```python
import jax
import jax.numpy as jnp
from jax import lax
from jax.experimental import pallas as pl
from jax.experimental.pallas import tpu as pltpu
from jax.sharding import PartitionSpec as P

RING = 8
FF_TILE = 256
D_TILE = 512


def local(tokens, router_probs, expert_ids, slot_expert, w_gate, w_up, w_down):
    tok_rows, width = tokens.shape
    top = expert_ids.shape[1]
    experts = slot_expert.shape[0]
    capacity = min(tok_rows, max(2, (tok_rows * top + experts - 1) // experts))
    gates = router_probs / jnp.sum(router_probs, axis=1, keepdims=True)
    flat_ids = expert_ids.reshape(-1)
    numbers = jnp.arange(experts, dtype=jnp.int32)
    slot_of = jnp.sum(
        jnp.where(slot_expert[None, :] == flat_ids[:, None], numbers[None, :], 0), axis=1
    )
    hits = (flat_ids[:, None] == numbers[None, :]).astype(jnp.int32)
    before = jnp.cumsum(hits, axis=0) - hits
    rank = jnp.sum(before * hits, axis=1)
    target = slot_of * capacity + rank
    select = (target[:, None] == jnp.arange(experts * capacity, dtype=jnp.int32)[None, :]).astype(
        jnp.float32
    )
    select = select.reshape(tok_rows, top, experts * capacity)
    spread = jnp.sum(select, axis=1).astype(jnp.bfloat16)
    weights_mix = jnp.einsum("tk,tkr->tr", gates, select)
    outgoing = jnp.einsum("tr,td->rd", spread, tokens, preferred_element_type=jnp.float32).astype(
        jnp.bfloat16
    )
    outgoing = outgoing.reshape(experts, capacity, width)
    arrived = lax.all_to_all(outgoing, "expert", split_axis=0, concat_axis=0, tiled=True)
    both = lax.all_gather(arrived, "sub", axis=0, tiled=True).reshape(-1, width)
    gate_in = jnp.dot(both, w_gate[0], preferred_element_type=jnp.float32)
    up_in = jnp.dot(both, w_up[0], preferred_element_type=jnp.float32)
    hidden = (jax.nn.silu(gate_in) * up_in).astype(jnp.bfloat16)
    summed = lax.psum_scatter(
        jnp.dot(hidden, w_down[0], preferred_element_type=jnp.float32).astype(jnp.bfloat16),
        "sub",
        scatter_dimension=0,
        tiled=True,
    )
    returned = lax.all_to_all(
        summed.reshape(experts, capacity, width), "expert", split_axis=0, concat_axis=0, tiled=True
    )
    outputs = returned.reshape(experts * capacity, width)
    weight_high = weights_mix.astype(jnp.bfloat16)
    weight_low = (weights_mix - weight_high.astype(jnp.float32)).astype(jnp.bfloat16)
    mixed = jnp.dot(weight_high, outputs, preferred_element_type=jnp.float32)
    mixed = mixed + jnp.dot(weight_low, outputs, preferred_element_type=jnp.float32)
    return mixed.astype(jnp.bfloat16)


def ring_place(e):
    z, x, core = lax.div(e, 4), lax.rem(lax.div(e, 2), 2), lax.rem(e, 2)
    return x * (RING - 1 - z) + (1 - x) * z, core


def ring_index(place, core):
    x = lax.div(place, RING // 2)
    z = x * (RING - 1 - place) + (1 - x) * place
    return z * 4 + x * 2 + core


def long_slot(s):
    return 2 * s - 1 if s else 0


def short_slot(s):
    return 2 * s


def other_slot(slot):
    if slot in (0, RING - 1):
        return slot
    return slot + 1 if slot % 2 else slot - 1


def kernel(
    tokens, probs, ids, slots, w_gate, w_up, w_down, out,
    x, mix, vg, vu, vd, hidden, own, away, near, long_out, long_in, short_out, short_in,
    w_sem, ag_send, ag_recv, sib_send, sib_recv, near_send, near_recv,
    long_send, long_recv, short_send, short_recv,
):
    rows, width = tokens.shape
    half = rows // 2
    ff = hidden.shape[1]
    me = lax.axis_index("expert")
    place, core = ring_place(me)
    step = 1 - 2 * core
    ahead = ring_index(lax.rem(place + step + RING, RING), core)
    behind = ring_index(lax.rem(place - step + RING, RING), core)
    sibling = me + step

    def device(e):
        return (lax.axis_index("groups"), e, lax.axis_index("sub"))

    def remote(src, dst, send, recv, e):
        return pltpu.make_async_remote_copy(
            src_ref=src, dst_ref=dst, send_sem=send, recv_sem=recv,
            device_id=device(e), device_id_type=pl.DeviceIdType.MESH,
        )

    barrier = pltpu.get_barrier_semaphore()
    for e in (ahead, behind, sibling):
        pl.semaphore_signal(barrier, inc=1, device_id=device(e), device_id_type=pl.DeviceIdType.MESH)

    loads = [
        pltpu.make_async_copy(w_gate.at[0], vg, w_sem.at[0]),
        pltpu.make_async_copy(w_up.at[0], vu, w_sem.at[1]),
        pltpu.make_async_copy(w_down.at[0], vd, w_sem.at[2]),
    ]
    for load in loads:
        load.start()

    x[0:rows, :] = tokens[...]
    p = probs[...]
    gates = p / jnp.sum(p, axis=0, keepdims=True)
    experts = mix.shape[2]
    number = lax.broadcasted_iota(jnp.int32, (experts, rows), 0)
    held = jnp.zeros((experts, rows), jnp.int32)
    for j in range(experts):
        held = jnp.where(number == j, slots[j], held)
    weight = jnp.zeros((experts, rows), jnp.float32)
    for k in range(p.shape[0]):
        weight = weight + jnp.where(ids[k:k + 1, :] == held, gates[k:k + 1, :], 0.0)
    mix[0, 0, :, 0:rows] = weight
    mix[0, 0, :, rows:] = jnp.zeros((experts, mix.shape[3] - rows), jnp.float32)

    pl.semaphore_wait(barrier, 3)

    def view(slot, side, part):
        if part == 2:
            return mix.at[slot, side]
        return x.at[pl.ds(slot * 2 * rows + side * rows + part * half, half), :]

    PARTS = (2, 0, 1)
    sends = []

    def ring_copy(src, dst, part, e):
        return remote(view(src, 0, part), view(dst, 0, part), ag_send.at[dst, part], ag_recv.at[dst, part], e)

    def sib_copy(slot, part):
        dst = other_slot(slot)
        return remote(view(slot, 0, part), view(dst, 1, part), sib_send.at[dst, part], sib_recv.at[dst, part], sibling)

    def start(copy):
        copy.start()
        sends.append(copy)

    for part in PARTS:
        start(ring_copy(0, long_slot(1), part, ahead))
        start(ring_copy(0, short_slot(1), part, behind))
    for part in PARTS:
        start(sib_copy(0, part))

    def await_sib(slot, part):
        remote(view(other_slot(slot), 0, part), view(slot, 1, part), sib_send.at[slot, part], sib_recv.at[slot, part], sibling).wait_recv()

    def arrive(s, parts):
        for part in parts:
            ring_copy(long_slot(s - 1), long_slot(s), part, ahead).wait_recv()
            if s < RING // 2:
                start(ring_copy(long_slot(s), long_slot(s + 1), part, ahead))
            start(sib_copy(long_slot(s), part))
            if s < RING // 2:
                ring_copy(short_slot(s - 1), short_slot(s), part, behind).wait_recv()
                if s < RING // 2 - 1:
                    start(ring_copy(short_slot(s), short_slot(s + 1), part, behind))
                start(sib_copy(short_slot(s), part))

    def first_half(group):
        for slot in group:
            for part in PARTS:
                await_sib(slot, part)
        base, count = group[0] * 2 * rows, len(group) * 2 * rows

        @pl.loop(0, ff // FF_TILE)
        def _(j):
            cols = pl.ds(pl.multiple_of(j * FF_TILE, FF_TILE), FF_TILE)
            a = x[base:base + count, :]
            g = jnp.dot(a, vg[:, cols], preferred_element_type=jnp.float32)
            u = jnp.dot(a, vu[:, cols], preferred_element_type=jnp.float32)
            hidden[0:count, cols] = (g / (1.0 + jnp.exp(-g)) * u).astype(jnp.bfloat16)

    def column(slot, side):
        table = mix[slot, side]
        row = lax.broadcasted_iota(jnp.int32, table.shape, 0)
        line = jnp.sum(jnp.where(row == me, table, 0.0), axis=0, keepdims=True)
        shape = (rows, table.shape[1])
        same = lax.broadcasted_iota(jnp.int32, shape, 0) == lax.broadcasted_iota(jnp.int32, shape, 1)
        return jnp.sum(jnp.where(same, line, 0.0), axis=1, keepdims=True)

    def near_copy(slot):
        dst = other_slot(slot)
        return remote(away.at[slot], near.at[dst], near_send.at[dst], near_recv.at[dst], sibling)

    def second_half(group):
        count = len(group) * 2 * rows
        scale = jnp.concatenate([column(slot, side) for slot in group for side in (0, 1)], axis=0)

        @pl.loop(0, width // D_TILE)
        def _(j):
            cols = pl.ds(pl.multiple_of(j * D_TILE, D_TILE), D_TILE)
            y = jnp.dot(hidden[0:count, :], vd[:, cols], preferred_element_type=jnp.float32)
            y = y.astype(jnp.bfloat16).astype(jnp.float32) * scale
            for i, slot in enumerate(group):
                own[slot, :, cols] = y[2 * i * rows:(2 * i + 1) * rows]
                away[slot, :, cols] = y[(2 * i + 1) * rows:(2 * i + 2) * rows].astype(jnp.bfloat16)

        for slot in group:
            start(near_copy(slot))

    def await_near(slot):
        remote(away.at[other_slot(slot)], near.at[slot], near_send.at[slot], near_recv.at[slot], sibling).wait_recv()

    groups = [[0]] + [[long_slot(s), short_slot(s)] for s in range(1, RING // 2)] + [[RING - 1]]

    for s in range(1, RING // 2 + 1):
        arrive(s, (2, 0))
        if s == 1:
            for load in loads:
                load.wait()
        first_half(groups[s - 1])
        arrive(s, (1,))
        second_half(groups[s - 1])

    def pass_on(k, far, slot_at, out_ref, in_ref, send, recv, e):
        slot = slot_at(far - k)
        if k == 0:
            await_near(slot)
        elif far - k:
            await_near(slot)
        for h in range(2):
            at = pl.ds(h * half, half)
            if k:
                remote(out_ref.at[k - 1, at, :], in_ref.at[k - 1, at, :], send.at[k - 1, h], recv.at[k - 1, h], e).wait_recv()
            total = own[slot, at, :] + near[slot, at, :].astype(jnp.float32)
            if k:
                total = total + in_ref[k - 1, at, :].astype(jnp.float32)
            out_ref[k, at, :] = total.astype(jnp.bfloat16)
            start(remote(out_ref.at[k, at, :], in_ref.at[k, at, :], send.at[k, h], recv.at[k, h], e))

    def pass_long(k):
        pass_on(k, RING // 2, long_slot, long_out, long_in, long_send, long_recv, behind)

    def pass_short(k):
        pass_on(k, RING // 2 - 1, short_slot, short_out, short_in, short_send, short_recv, ahead)

    pass_short(0)
    first_half(groups[-1])
    second_half(groups[-1])
    pass_long(0)
    for k in range(1, RING // 2 - 1):
        pass_short(k)
        pass_long(k)
    pass_long(RING // 2 - 1)

    await_near(0)
    last = RING // 2 - 1
    for h in range(2):
        at = pl.ds(h * half, half)
        remote(short_out.at[last - 1, at, :], short_in.at[last - 1, at, :], short_send.at[last - 1, h], short_recv.at[last - 1, h], ahead).wait_recv()
        remote(long_out.at[last, at, :], long_in.at[last, at, :], long_send.at[last, h], long_recv.at[last, h], behind).wait_recv()
        total = own[0, at, :] + near[0, at, :].astype(jnp.float32)
        total = total + short_in[last - 1, at, :].astype(jnp.float32) + long_in[last, at, :].astype(jnp.float32)
        out[at, :] = total.astype(jnp.bfloat16)
    for copy in sends:
        copy.wait_send()


def ring_local(tokens, router_probs, expert_ids, slot_expert, w_gate, w_up, w_down):
    rows, width = tokens.shape
    ff = w_gate.shape[2]
    experts = slot_expert.shape[0]
    hops = RING // 2
    bf16, f32 = jnp.bfloat16, jnp.float32
    dma = pltpu.SemaphoreType.DMA
    vmem = pl.BlockSpec(memory_space=pltpu.VMEM)
    hbm = pl.BlockSpec(memory_space=pl.ANY)
    return pl.pallas_call(
        kernel,
        out_shape=jax.ShapeDtypeStruct((rows, width), bf16),
        in_specs=[vmem, vmem, vmem, pl.BlockSpec(memory_space=pltpu.SMEM), hbm, hbm, hbm],
        out_specs=vmem,
        scratch_shapes=[
            pltpu.VMEM((RING * 2 * rows, width), bf16),
            pltpu.VMEM((RING, 2, experts, 128), f32),
            pltpu.VMEM((width, ff), bf16),
            pltpu.VMEM((width, ff), bf16),
            pltpu.VMEM((ff, width), bf16),
            pltpu.VMEM((4 * rows, ff), bf16),
            pltpu.VMEM((RING, rows, width), f32),
            pltpu.VMEM((RING, rows, width), bf16),
            pltpu.VMEM((RING, rows, width), bf16),
            pltpu.VMEM((hops, rows, width), bf16),
            pltpu.VMEM((hops, rows, width), bf16),
            pltpu.VMEM((hops - 1, rows, width), bf16),
            pltpu.VMEM((hops - 1, rows, width), bf16),
            dma((3,)),
            dma((RING, 3)), dma((RING, 3)), dma((RING, 3)), dma((RING, 3)),
            dma((RING,)), dma((RING,)),
            dma((hops, 2)), dma((hops, 2)), dma((hops - 1, 2)), dma((hops - 1, 2)),
        ],
        compiler_params=pltpu.CompilerParams(
            collective_id=0, has_side_effects=True, vmem_limit_bytes=50 * 2**20
        ),
        cost_estimate=pl.CostEstimate(
            flops=6 * RING * 2 * rows * width * ff, bytes_accessed=6 * width * ff, transcendentals=0
        ),
    )(tokens, router_probs.T, expert_ids.T, slot_expert, w_gate, w_up, w_down)


def solution(mesh):
    placed = (
        P(("groups", "expert", "sub"), None),
        P(("groups", "expert", "sub"), None),
        P(("groups", "expert", "sub"), None),
        P(),
        P("expert", None, "sub"),
        P("expert", None, "sub"),
        P("expert", "sub", None),
    )
    ring = mesh.shape["sub"] == 1 and mesh.shape["expert"] == 2 * RING
    return jax.shard_map(
        ring_local if ring else local,
        mesh=mesh,
        in_specs=placed,
        out_specs=P(("groups", "expert", "sub"), None),
        check_vma=False,
    )
```

```python
import functools

import jax
import jax.numpy as jnp
from jax import lax
from jax.experimental import pallas as pl
from jax.experimental.pallas import tpu as pltpu
from jax.sharding import PartitionSpec as P

RING = 8
PARTS = 2
FF_TILE = 256
D_TILE = 512


def local(tokens, router_probs, expert_ids, slot_expert, w_gate, w_up, w_down):
    tok_rows, width = tokens.shape
    top = expert_ids.shape[1]
    experts = slot_expert.shape[0]
    capacity = min(tok_rows, max(2, (tok_rows * top + experts - 1) // experts))
    gates = router_probs / jnp.sum(router_probs, axis=1, keepdims=True)
    flat_ids = expert_ids.reshape(-1)
    numbers = jnp.arange(experts, dtype=jnp.int32)
    slot_of = jnp.sum(
        jnp.where(slot_expert[None, :] == flat_ids[:, None], numbers[None, :], 0), axis=1
    )
    hits = (flat_ids[:, None] == numbers[None, :]).astype(jnp.int32)
    before = jnp.cumsum(hits, axis=0) - hits
    rank = jnp.sum(before * hits, axis=1)
    target = slot_of * capacity + rank
    select = (target[:, None] == jnp.arange(experts * capacity, dtype=jnp.int32)[None, :]).astype(
        jnp.float32
    )
    select = select.reshape(tok_rows, top, experts * capacity)
    spread = jnp.sum(select, axis=1).astype(jnp.bfloat16)
    weights_mix = jnp.einsum("tk,tkr->tr", gates, select)
    outgoing = jnp.einsum("tr,td->rd", spread, tokens, preferred_element_type=jnp.float32).astype(
        jnp.bfloat16
    )
    outgoing = outgoing.reshape(experts, capacity, width)
    arrived = lax.all_to_all(outgoing, "expert", split_axis=0, concat_axis=0, tiled=True)
    both = lax.all_gather(arrived, "sub", axis=0, tiled=True).reshape(-1, width)
    gate_in = jnp.dot(both, w_gate[0], preferred_element_type=jnp.float32)
    up_in = jnp.dot(both, w_up[0], preferred_element_type=jnp.float32)
    hidden = (jax.nn.silu(gate_in) * up_in).astype(jnp.bfloat16)
    summed = lax.psum_scatter(
        jnp.dot(hidden, w_down[0], preferred_element_type=jnp.float32).astype(jnp.bfloat16),
        "sub",
        scatter_dimension=0,
        tiled=True,
    )
    returned = lax.all_to_all(
        summed.reshape(experts, capacity, width), "expert", split_axis=0, concat_axis=0, tiled=True
    )
    outputs = returned.reshape(experts * capacity, width)
    weight_high = weights_mix.astype(jnp.bfloat16)
    weight_low = (weights_mix - weight_high.astype(jnp.float32)).astype(jnp.bfloat16)
    mixed = jnp.dot(weight_high, outputs, preferred_element_type=jnp.float32)
    mixed = mixed + jnp.dot(weight_low, outputs, preferred_element_type=jnp.float32)
    return mixed.astype(jnp.bfloat16)


def ring_place(e):
    z, x, core = lax.div(e, 4), lax.rem(lax.div(e, 2), 2), lax.rem(e, 2)
    return x * (RING - 1 - z) + (1 - x) * z, core


def ring_index(place, core):
    x = lax.div(place, RING // 2)
    z = x * (RING - 1 - place) + (1 - x) * place
    return z * 4 + x * 2 + core


def long_slot(s):
    return 2 * s - 1 if s else 0


def short_slot(s):
    return 2 * s


def other_slot(slot):
    if slot in (0, RING - 1):
        return slot
    return slot + 1 if slot % 2 else slot - 1


def kernel(
    tokens, probs_in, ids_in, slots_in, w_gate, w_up, w_down, out,
    probs, ids, slots, x, mix, vg, vu, vd, hidden, own, away, near, long_out, long_in, short_out, short_in,
    in_sem, w_sem, ag_send, ag_recv, sib_send, sib_recv, near_send, near_recv,
    long_send, long_recv, short_send, short_recv,
):
    rows, width = tokens.shape
    half = rows // PARTS
    ff = hidden.shape[1]
    me = lax.axis_index("expert")
    place, core = ring_place(me)
    step = 1 - 2 * core
    ahead = ring_index(lax.rem(place + step + RING, RING), core)
    behind = ring_index(lax.rem(place - step + RING, RING), core)
    sibling = me + step

    def device(e):
        return (lax.axis_index("groups"), e, lax.axis_index("sub"))

    def remote(src, dst, send, recv, e):
        return pltpu.make_async_remote_copy(
            src_ref=src, dst_ref=dst, send_sem=send, recv_sem=recv,
            device_id=device(e), device_id_type=pl.DeviceIdType.MESH,
        )

    barrier = pltpu.get_barrier_semaphore()
    for e in (ahead, behind, sibling):
        pl.semaphore_signal(barrier, inc=1, device_id=device(e), device_id_type=pl.DeviceIdType.MESH)

    smalls = [
        pltpu.make_async_copy(probs_in, probs, in_sem.at[0]),
        pltpu.make_async_copy(ids_in, ids, in_sem.at[1]),
        pltpu.make_async_copy(slots_in, slots, in_sem.at[2]),
    ]
    loads = [
        pltpu.make_async_copy(tokens, x.at[pl.ds(0, rows), :], w_sem.at[0]),
        pltpu.make_async_copy(w_gate.at[0], vg, w_sem.at[1]),
        pltpu.make_async_copy(w_up.at[0], vu, w_sem.at[2]),
        pltpu.make_async_copy(w_down.at[0], vd, w_sem.at[3]),
    ]
    for load in smalls:
        load.start()

    pl.semaphore_wait(barrier, 3)

    def view(slot, side, part):
        if part == PARTS:
            return mix.at[slot, side]
        return x.at[pl.ds(slot * 2 * rows + side * rows + part * half, half), :]

    def held_at(slot, part):
        if slot == 0 and part < PARTS:
            return tokens.at[pl.ds(part * half, half), :]
        return view(slot, 0, part)

    sends = []

    def ring_copy(src, dst, part, e):
        return remote(held_at(src, part), view(dst, 0, part), ag_send.at[dst, part], ag_recv.at[dst, part], e)

    def sib_copy(slot, part):
        dst = other_slot(slot)
        return remote(held_at(slot, part), view(dst, 1, part), sib_send.at[dst, part], sib_recv.at[dst, part], sibling)

    def start(copy):
        copy.start()
        sends.append(copy)

    for part in range(PARTS):
        start(ring_copy(0, long_slot(1), part, ahead))
        start(ring_copy(0, short_slot(1), part, behind))
    for part in range(PARTS):
        start(sib_copy(0, part))
    for load in loads:
        load.start()
    for load in smalls:
        load.wait()

    p = probs[...]
    gates = p / jnp.sum(p, axis=0, keepdims=True)
    experts = mix.shape[2]
    number = lax.broadcasted_iota(jnp.int32, (experts, rows), 0)
    held = jnp.zeros((experts, rows), jnp.int32)
    for j in range(experts):
        held = jnp.where(number == j, slots[j], held)
    weight = jnp.zeros((experts, rows), jnp.float32)
    for k in range(p.shape[0]):
        weight = weight + jnp.where(ids[k:k + 1, :] == held, gates[k:k + 1, :], 0.0)
    mix[0, 0, :, 0:rows] = weight
    mix[0, 0, :, rows:] = jnp.zeros((experts, mix.shape[3] - rows), jnp.float32)
    start(ring_copy(0, long_slot(1), PARTS, ahead))
    start(ring_copy(0, short_slot(1), PARTS, behind))
    start(sib_copy(0, PARTS))

    def await_sib(slot, part):
        remote(held_at(other_slot(slot), part), view(slot, 1, part), sib_send.at[slot, part], sib_recv.at[slot, part], sibling).wait_recv()

    def arrive(s, parts):
        for part in parts:
            ring_copy(long_slot(s - 1), long_slot(s), part, ahead).wait_recv()
            if s < RING // 2:
                start(ring_copy(long_slot(s), long_slot(s + 1), part, ahead))
            start(sib_copy(long_slot(s), part))
            if s < RING // 2:
                ring_copy(short_slot(s - 1), short_slot(s), part, behind).wait_recv()
                if s < RING // 2 - 1:
                    start(ring_copy(short_slot(s), short_slot(s + 1), part, behind))
                start(sib_copy(short_slot(s), part))

    def first_items(group):
        base, count = group[0] * 2 * rows, len(group) * 2 * rows

        def ready():
            for slot in group:
                for part in range(PARTS):
                    await_sib(slot, part)

        def tile(j):
            if j == 0:
                ready()
            cols = pl.ds(j * FF_TILE, FF_TILE)
            a = x[base:base + count, :]
            g = jnp.dot(a, vg[:, cols], preferred_element_type=jnp.float32)
            u = jnp.dot(a, vu[:, cols], preferred_element_type=jnp.float32)
            hidden[0:count, cols] = (g / (1.0 + jnp.exp(-g)) * u).astype(jnp.bfloat16)

        return [functools.partial(tile, j) for j in range(ff // FF_TILE)]

    def column(slot, side):
        table = mix[slot, side]
        row = lax.broadcasted_iota(jnp.int32, table.shape, 0)
        line = jnp.sum(jnp.where(row == me, table, 0.0), axis=0, keepdims=True)
        shape = (rows, table.shape[1])
        same = lax.broadcasted_iota(jnp.int32, shape, 0) == lax.broadcasted_iota(jnp.int32, shape, 1)
        return jnp.sum(jnp.where(same, line, 0.0), axis=1, keepdims=True)

    def near_copy(slot):
        dst = other_slot(slot)
        return remote(away.at[slot], near.at[dst], near_send.at[dst], near_recv.at[dst], sibling)

    def second_items(group):
        count = len(group) * 2 * rows
        scale = []

        def tile(j):
            if j == 0:
                for slot in group:
                    await_sib(slot, PARTS)
                scale.append(jnp.concatenate([column(slot, side) for slot in group for side in (0, 1)], axis=0))
            cols = pl.ds(j * D_TILE, D_TILE)
            y = jnp.dot(hidden[0:count, :], vd[:, cols], preferred_element_type=jnp.float32)
            y = y.astype(jnp.bfloat16).astype(jnp.float32) * scale[0]
            for i, slot in enumerate(group):
                own[slot, :, cols] = y[2 * i * rows:(2 * i + 1) * rows]
                away[slot, :, cols] = y[(2 * i + 1) * rows:(2 * i + 2) * rows].astype(jnp.bfloat16)
            if j == width // D_TILE - 1:
                for slot in group:
                    start(near_copy(slot))

        return [functools.partial(tile, j) for j in range(width // D_TILE)]

    def await_near(slot):
        remote(away.at[other_slot(slot)], near.at[slot], near_send.at[slot], near_recv.at[slot], sibling).wait_recv()

    groups = [[0]] + [[long_slot(s), short_slot(s)] for s in range(1, RING // 2)] + [[RING - 1]]

    for s in range(1, RING // 2 + 1):
        items = first_items(groups[s - 1]) + second_items(groups[s - 1])
        for part in range(PARTS):
            arrive(s, (part,) if part else (part, PARTS))
            if s == 1 and part == 0:
                for load in loads:
                    load.wait()
            for item in items[len(items) * part // PARTS:len(items) * (part + 1) // PARTS]:
                item()

    def pass_on(k, far, slot_at, out_ref, in_ref, send, recv, e):
        slot = slot_at(far - k)
        if k == 0:
            await_near(slot)
        elif far - k:
            await_near(slot)
        for h in range(PARTS):
            at = pl.ds(h * half, half)
            if k:
                remote(out_ref.at[k - 1, at, :], in_ref.at[k - 1, at, :], send.at[k - 1, h], recv.at[k - 1, h], e).wait_recv()
            total = own[slot, at, :] + near[slot, at, :].astype(jnp.float32)
            if k:
                total = total + in_ref[k - 1, at, :].astype(jnp.float32)
            out_ref[k, at, :] = total.astype(jnp.bfloat16)
            start(remote(out_ref.at[k, at, :], in_ref.at[k, at, :], send.at[k, h], recv.at[k, h], e))

    def pass_long(k):
        pass_on(k, RING // 2, long_slot, long_out, long_in, long_send, long_recv, behind)

    def pass_short(k):
        pass_on(k, RING // 2 - 1, short_slot, short_out, short_in, short_send, short_recv, ahead)

    pass_short(0)
    for item in first_items(groups[-1]) + second_items(groups[-1]):
        item()
    pass_long(0)
    for k in range(1, RING // 2 - 1):
        pass_short(k)
        pass_long(k)
    pass_long(RING // 2 - 1)

    await_near(0)
    last = RING // 2 - 1
    for h in range(PARTS):
        at = pl.ds(h * half, half)
        remote(short_out.at[last - 1, at, :], short_in.at[last - 1, at, :], short_send.at[last - 1, h], short_recv.at[last - 1, h], ahead).wait_recv()
        remote(long_out.at[last, at, :], long_in.at[last, at, :], long_send.at[last, h], long_recv.at[last, h], behind).wait_recv()
        total = own[0, at, :] + near[0, at, :].astype(jnp.float32)
        total = total + short_in[last - 1, at, :].astype(jnp.float32) + long_in[last, at, :].astype(jnp.float32)
        out[at, :] = total.astype(jnp.bfloat16)
    for copy in sends:
        copy.wait_send()


def ring_local(tokens, router_probs, expert_ids, slot_expert, w_gate, w_up, w_down):
    rows, width = tokens.shape
    ff = w_gate.shape[2]
    experts = slot_expert.shape[0]
    hops = RING // 2
    bf16, f32 = jnp.bfloat16, jnp.float32
    dma = pltpu.SemaphoreType.DMA
    vmem = pl.BlockSpec(memory_space=pltpu.VMEM)
    hbm = pl.BlockSpec(memory_space=pl.ANY)
    return pl.pallas_call(
        kernel,
        out_shape=jax.ShapeDtypeStruct((rows, width), bf16),
        in_specs=[hbm] * 7,
        out_specs=vmem,
        scratch_shapes=[
            pltpu.VMEM(router_probs.shape[::-1], f32),
            pltpu.VMEM(expert_ids.shape[::-1], jnp.int32),
            pltpu.SMEM(slot_expert.shape, jnp.int32),
            pltpu.VMEM((RING * 2 * rows, width), bf16),
            pltpu.VMEM((RING, 2, experts, 128), f32),
            pltpu.VMEM((width, ff), bf16),
            pltpu.VMEM((width, ff), bf16),
            pltpu.VMEM((ff, width), bf16),
            pltpu.VMEM((4 * rows, ff), bf16),
            pltpu.VMEM((RING, rows, width), f32),
            pltpu.VMEM((RING, rows, width), bf16),
            pltpu.VMEM((RING, rows, width), bf16),
            pltpu.VMEM((hops, rows, width), bf16),
            pltpu.VMEM((hops, rows, width), bf16),
            pltpu.VMEM((hops - 1, rows, width), bf16),
            pltpu.VMEM((hops - 1, rows, width), bf16),
            dma((3,)), dma((4,)),
            dma((RING, PARTS + 1)), dma((RING, PARTS + 1)), dma((RING, PARTS + 1)), dma((RING, PARTS + 1)),
            dma((RING,)), dma((RING,)),
            dma((hops, PARTS)), dma((hops, PARTS)), dma((hops - 1, PARTS)), dma((hops - 1, PARTS)),
        ],
        compiler_params=pltpu.CompilerParams(
            collective_id=0, has_side_effects=True, vmem_limit_bytes=60 * 2**20
        ),
        cost_estimate=pl.CostEstimate(
            flops=6 * RING * 2 * rows * width * ff, bytes_accessed=6 * width * ff, transcendentals=0
        ),
    )(tokens, router_probs.T, expert_ids.T, slot_expert, w_gate, w_up, w_down)


def solution(mesh):
    placed = (
        P(("groups", "expert", "sub"), None),
        P(("groups", "expert", "sub"), None),
        P(("groups", "expert", "sub"), None),
        P(),
        P("expert", None, "sub"),
        P("expert", None, "sub"),
        P("expert", "sub", None),
    )
    ring = mesh.shape["sub"] == 1 and mesh.shape["expert"] == 2 * RING
    return jax.shard_map(
        ring_local if ring else local,
        mesh=mesh,
        in_specs=placed,
        out_specs=P(("groups", "expert", "sub"), None),
        check_vma=False,
    )
```

```python
import functools

import jax
import jax.numpy as jnp
from jax import lax
from jax.experimental import pallas as pl
from jax.experimental.pallas import tpu as pltpu
from jax.sharding import PartitionSpec as P

RING = 8
PARTS = 2
FF_TILE = 256
D_TILE = 512


def local(tokens, router_probs, expert_ids, slot_expert, w_gate, w_up, w_down):
    tok_rows, width = tokens.shape
    top = expert_ids.shape[1]
    experts = slot_expert.shape[0]
    capacity = min(tok_rows, max(2, (tok_rows * top + experts - 1) // experts))
    gates = router_probs / jnp.sum(router_probs, axis=1, keepdims=True)
    flat_ids = expert_ids.reshape(-1)
    numbers = jnp.arange(experts, dtype=jnp.int32)
    slot_of = jnp.sum(
        jnp.where(slot_expert[None, :] == flat_ids[:, None], numbers[None, :], 0), axis=1
    )
    hits = (flat_ids[:, None] == numbers[None, :]).astype(jnp.int32)
    before = jnp.cumsum(hits, axis=0) - hits
    rank = jnp.sum(before * hits, axis=1)
    target = slot_of * capacity + rank
    select = (target[:, None] == jnp.arange(experts * capacity, dtype=jnp.int32)[None, :]).astype(
        jnp.float32
    )
    select = select.reshape(tok_rows, top, experts * capacity)
    spread = jnp.sum(select, axis=1).astype(jnp.bfloat16)
    weights_mix = jnp.einsum("tk,tkr->tr", gates, select)
    outgoing = jnp.einsum("tr,td->rd", spread, tokens, preferred_element_type=jnp.float32).astype(
        jnp.bfloat16
    )
    outgoing = outgoing.reshape(experts, capacity, width)
    arrived = lax.all_to_all(outgoing, "expert", split_axis=0, concat_axis=0, tiled=True)
    both = lax.all_gather(arrived, "sub", axis=0, tiled=True).reshape(-1, width)
    gate_in = jnp.dot(both, w_gate[0], preferred_element_type=jnp.float32)
    up_in = jnp.dot(both, w_up[0], preferred_element_type=jnp.float32)
    hidden = (jax.nn.silu(gate_in) * up_in).astype(jnp.bfloat16)
    summed = lax.psum_scatter(
        jnp.dot(hidden, w_down[0], preferred_element_type=jnp.float32).astype(jnp.bfloat16),
        "sub",
        scatter_dimension=0,
        tiled=True,
    )
    returned = lax.all_to_all(
        summed.reshape(experts, capacity, width), "expert", split_axis=0, concat_axis=0, tiled=True
    )
    outputs = returned.reshape(experts * capacity, width)
    weight_high = weights_mix.astype(jnp.bfloat16)
    weight_low = (weights_mix - weight_high.astype(jnp.float32)).astype(jnp.bfloat16)
    mixed = jnp.dot(weight_high, outputs, preferred_element_type=jnp.float32)
    mixed = mixed + jnp.dot(weight_low, outputs, preferred_element_type=jnp.float32)
    return mixed.astype(jnp.bfloat16)


def ring_place(e):
    z, x, core = lax.div(e, 4), lax.rem(lax.div(e, 2), 2), lax.rem(e, 2)
    return x * (RING - 1 - z) + (1 - x) * z, core


def ring_index(place, core):
    x = lax.div(place, RING // 2)
    z = x * (RING - 1 - place) + (1 - x) * place
    return z * 4 + x * 2 + core


def long_slot(s):
    return 2 * s - 1 if s else 0


def short_slot(s):
    return 2 * s


def other_slot(slot):
    if slot in (0, RING - 1):
        return slot
    return slot + 1 if slot % 2 else slot - 1


def kernel(
    tokens, probs_in, ids_in, slots_in, w_gate, w_up, w_down, out, last_in,
    probs, ids, slots, x, mix, vg, vu, vd, hidden, own, away, near, long_out, long_in, short_out, short_in,
    in_sem, w_sem, ag_send, ag_recv, sib_send, sib_recv, near_send, near_recv,
    long_send, long_recv, short_send, short_recv,
    rest, out_sem,
):
    rows, width = tokens.shape
    half = rows // PARTS
    ff = hidden.shape[1]
    me = lax.axis_index("expert")
    place, core = ring_place(me)
    step = 1 - 2 * core
    ahead = ring_index(lax.rem(place + step + RING, RING), core)
    behind = ring_index(lax.rem(place - step + RING, RING), core)
    sibling = me + step

    def device(e):
        return (lax.axis_index("groups"), e, lax.axis_index("sub"))

    def remote(src, dst, send, recv, e):
        return pltpu.make_async_remote_copy(
            src_ref=src, dst_ref=dst, send_sem=send, recv_sem=recv,
            device_id=device(e), device_id_type=pl.DeviceIdType.MESH,
        )

    barrier = pltpu.get_barrier_semaphore()
    for e in (ahead, behind, sibling):
        pl.semaphore_signal(barrier, inc=1, device_id=device(e), device_id_type=pl.DeviceIdType.MESH)

    smalls = [
        pltpu.make_async_copy(probs_in, probs, in_sem.at[0]),
        pltpu.make_async_copy(ids_in, ids, in_sem.at[1]),
        pltpu.make_async_copy(slots_in, slots, in_sem.at[2]),
    ]
    loads = [
        pltpu.make_async_copy(tokens, x.at[pl.ds(0, rows), :], w_sem.at[0]),
        pltpu.make_async_copy(w_gate.at[0], vg, w_sem.at[1]),
        pltpu.make_async_copy(w_up.at[0], vu, w_sem.at[2]),
        pltpu.make_async_copy(w_down.at[0], vd, w_sem.at[3]),
    ]
    for load in smalls:
        load.start()

    pl.semaphore_wait(barrier, 3)

    def view(slot, side, part):
        if part == PARTS:
            return mix.at[slot, side]
        return x.at[pl.ds(slot * 2 * rows + side * rows + part * half, half), :]

    def held_at(slot, part):
        if slot == 0 and part < PARTS:
            return tokens.at[pl.ds(part * half, half), :]
        return view(slot, 0, part)

    sends, stores = [], []

    def ring_copy(src, dst, part, e):
        return remote(held_at(src, part), view(dst, 0, part), ag_send.at[dst, part], ag_recv.at[dst, part], e)

    def sib_copy(slot, part):
        dst = other_slot(slot)
        return remote(held_at(slot, part), view(dst, 1, part), sib_send.at[dst, part], sib_recv.at[dst, part], sibling)

    def start(copy):
        copy.start()
        sends.append(copy)

    for part in range(PARTS):
        start(ring_copy(0, long_slot(1), part, ahead))
        start(ring_copy(0, short_slot(1), part, behind))
    for part in range(PARTS):
        start(sib_copy(0, part))
    for load in loads:
        load.start()
    for load in smalls:
        load.wait()

    p = probs[...]
    gates = p / jnp.sum(p, axis=0, keepdims=True)
    experts = mix.shape[2]
    number = lax.broadcasted_iota(jnp.int32, (experts, rows), 0)
    held = jnp.zeros((experts, rows), jnp.int32)
    for j in range(experts):
        held = jnp.where(number == j, slots[j], held)
    weight = jnp.zeros((experts, rows), jnp.float32)
    for k in range(p.shape[0]):
        weight = weight + jnp.where(ids[k:k + 1, :] == held, gates[k:k + 1, :], 0.0)
    mix[0, 0, :, 0:rows] = weight
    mix[0, 0, :, rows:] = jnp.zeros((experts, mix.shape[3] - rows), jnp.float32)
    start(ring_copy(0, long_slot(1), PARTS, ahead))
    start(ring_copy(0, short_slot(1), PARTS, behind))
    start(sib_copy(0, PARTS))

    def await_sib(slot, part):
        remote(held_at(other_slot(slot), part), view(slot, 1, part), sib_send.at[slot, part], sib_recv.at[slot, part], sibling).wait_recv()

    def arrive(s, parts):
        for part in parts:
            ring_copy(long_slot(s - 1), long_slot(s), part, ahead).wait_recv()
            if s < RING // 2:
                start(ring_copy(long_slot(s), long_slot(s + 1), part, ahead))
            start(sib_copy(long_slot(s), part))
            if s < RING // 2:
                ring_copy(short_slot(s - 1), short_slot(s), part, behind).wait_recv()
                if s < RING // 2 - 1:
                    start(ring_copy(short_slot(s), short_slot(s + 1), part, behind))
                start(sib_copy(short_slot(s), part))

    def first_items(group):
        base, count = group[0] * 2 * rows, len(group) * 2 * rows

        def ready():
            for slot in group:
                for part in range(PARTS):
                    await_sib(slot, part)

        def tile(j):
            if j == 0:
                ready()
            cols = pl.ds(j * FF_TILE, FF_TILE)
            a = x[base:base + count, :]
            g = jnp.dot(a, vg[:, cols], preferred_element_type=jnp.float32)
            u = jnp.dot(a, vu[:, cols], preferred_element_type=jnp.float32)
            hidden[0:count, cols] = (g / (1.0 + jnp.exp(-g)) * u).astype(jnp.bfloat16)

        return [functools.partial(tile, j) for j in range(ff // FF_TILE)]

    def column(slot, side):
        table = mix[slot, side]
        row = lax.broadcasted_iota(jnp.int32, table.shape, 0)
        line = jnp.sum(jnp.where(row == me, table, 0.0), axis=0, keepdims=True)
        shape = (rows, table.shape[1])
        same = lax.broadcasted_iota(jnp.int32, shape, 0) == lax.broadcasted_iota(jnp.int32, shape, 1)
        return jnp.sum(jnp.where(same, line, 0.0), axis=1, keepdims=True)

    def near_copy(slot):
        dst = other_slot(slot)
        return remote(away.at[slot], near.at[dst], near_send.at[dst], near_recv.at[dst], sibling)

    def second_items(group):
        count = len(group) * 2 * rows
        scale = []

        def tile(j):
            if j == 0:
                for slot in group:
                    await_sib(slot, PARTS)
                scale.append(jnp.concatenate([column(slot, side) for slot in group for side in (0, 1)], axis=0))
            cols = pl.ds(j * D_TILE, D_TILE)
            y = jnp.dot(hidden[0:count, :], vd[:, cols], preferred_element_type=jnp.float32)
            y = y.astype(jnp.bfloat16).astype(jnp.float32) * scale[0]
            for i, slot in enumerate(group):
                own[slot, :, cols] = y[2 * i * rows:(2 * i + 1) * rows]
                away[slot, :, cols] = y[(2 * i + 1) * rows:(2 * i + 2) * rows].astype(jnp.bfloat16)
            if j == width // D_TILE - 1:
                for slot in group:
                    start(near_copy(slot))

        return [functools.partial(tile, j) for j in range(width // D_TILE)]

    def await_near(slot):
        remote(away.at[other_slot(slot)], near.at[slot], near_send.at[slot], near_recv.at[slot], sibling).wait_recv()

    groups = [[0]] + [[long_slot(s), short_slot(s)] for s in range(1, RING // 2)] + [[RING - 1]]

    for s in range(1, RING // 2 + 1):
        items = first_items(groups[s - 1]) + second_items(groups[s - 1])
        for part in range(PARTS):
            arrive(s, (part,) if part else (part, PARTS))
            if s == 1 and part == 0:
                for load in loads:
                    load.wait()
            for item in items[len(items) * part // PARTS:len(items) * (part + 1) // PARTS]:
                item()

    def pass_on(k, far, slot_at, out_ref, in_ref, send, recv, e):
        slot = slot_at(far - k)
        if k == 0:
            await_near(slot)
        elif far - k:
            await_near(slot)
        for h in range(PARTS):
            at = pl.ds(h * half, half)
            if k:
                remote(out_ref.at[k - 1, at, :], in_ref.at[k - 1, at, :], send.at[k - 1, h], recv.at[k - 1, h], e).wait_recv()
            total = own[slot, at, :] + near[slot, at, :].astype(jnp.float32)
            if k:
                total = total + in_ref[k - 1, at, :].astype(jnp.float32)
            out_ref[k, at, :] = total.astype(jnp.bfloat16)
            landing = last_in.at[at, :] if k == RING // 2 - 1 else in_ref.at[k, at, :]
            start(remote(out_ref.at[k, at, :], landing, send.at[k, h], recv.at[k, h], e))

    def pass_long(k):
        pass_on(k, RING // 2, long_slot, long_out, long_in, long_send, long_recv, behind)

    def pass_short(k):
        pass_on(k, RING // 2 - 1, short_slot, short_out, short_in, short_send, short_recv, ahead)

    for item in first_items(groups[-1]):
        item()
    pass_short(0)
    for item in second_items(groups[-1]):
        item()
    pass_long(0)
    for k in range(1, RING // 2 - 1):
        pass_short(k)
        pass_long(k)
    pass_long(RING // 2 - 1)

    await_near(0)
    last = RING // 2 - 1
    for h in range(PARTS):
        at = pl.ds(h * half, half)
        remote(short_out.at[last - 1, at, :], short_in.at[last - 1, at, :], short_send.at[last - 1, h], short_recv.at[last - 1, h], ahead).wait_recv()
        total = own[0, at, :] + near[0, at, :].astype(jnp.float32)
        rest[at, :] = total + short_in[last - 1, at, :].astype(jnp.float32)
        store = pltpu.make_async_copy(rest.at[at, :], out.at[at, :], out_sem.at[h])
        store.start()
        stores.append(store)
    for h in range(PARTS):
        at = pl.ds(h * half, half)
        remote(long_out.at[last, at, :], last_in.at[at, :], long_send.at[last, h], long_recv.at[last, h], behind).wait_recv()
    for store in stores:
        store.wait()
    for copy in sends:
        copy.wait_send()


def ring_local(tokens, router_probs, expert_ids, slot_expert, w_gate, w_up, w_down):
    rows, width = tokens.shape
    ff = w_gate.shape[2]
    experts = slot_expert.shape[0]
    hops = RING // 2
    bf16, f32 = jnp.bfloat16, jnp.float32
    dma = pltpu.SemaphoreType.DMA
    hbm = pl.BlockSpec(memory_space=pl.ANY)
    here, arrived = pl.pallas_call(
        kernel,
        out_shape=(jax.ShapeDtypeStruct((rows, width), f32), jax.ShapeDtypeStruct((rows, width), bf16)),
        in_specs=[hbm] * 7,
        out_specs=(hbm, hbm),
        scratch_shapes=[
            pltpu.VMEM(router_probs.shape[::-1], f32),
            pltpu.VMEM(expert_ids.shape[::-1], jnp.int32),
            pltpu.SMEM(slot_expert.shape, jnp.int32),
            pltpu.VMEM((RING * 2 * rows, width), bf16),
            pltpu.VMEM((RING, 2, experts, 128), f32),
            pltpu.VMEM((width, ff), bf16),
            pltpu.VMEM((width, ff), bf16),
            pltpu.VMEM((ff, width), bf16),
            pltpu.VMEM((4 * rows, ff), bf16),
            pltpu.VMEM((RING, rows, width), f32),
            pltpu.VMEM((RING, rows, width), bf16),
            pltpu.VMEM((RING, rows, width), bf16),
            pltpu.VMEM((hops, rows, width), bf16),
            pltpu.VMEM((hops - 1, rows, width), bf16),
            pltpu.VMEM((hops - 1, rows, width), bf16),
            pltpu.VMEM((hops - 1, rows, width), bf16),
            dma((3,)), dma((4,)),
            dma((RING, PARTS + 1)), dma((RING, PARTS + 1)), dma((RING, PARTS + 1)), dma((RING, PARTS + 1)),
            dma((RING,)), dma((RING,)),
            dma((hops, PARTS)), dma((hops, PARTS)), dma((hops - 1, PARTS)), dma((hops - 1, PARTS)),
            pltpu.VMEM((rows, width), f32), dma((PARTS,)),
        ],
        compiler_params=pltpu.CompilerParams(
            collective_id=0, has_side_effects=True, vmem_limit_bytes=60 * 2**20
        ),
        cost_estimate=pl.CostEstimate(
            flops=6 * RING * 2 * rows * width * ff, bytes_accessed=6 * width * ff, transcendentals=0
        ),
    )(tokens, router_probs.T, expert_ids.T, slot_expert, w_gate, w_up, w_down)
    return (here + arrived.astype(f32)).astype(bf16)


def solution(mesh):
    placed = (
        P(("groups", "expert", "sub"), None),
        P(("groups", "expert", "sub"), None),
        P(("groups", "expert", "sub"), None),
        P(),
        P("expert", None, "sub"),
        P("expert", None, "sub"),
        P("expert", "sub", None),
    )
    ring = mesh.shape["sub"] == 1 and mesh.shape["expert"] == 2 * RING
    return jax.shard_map(
        ring_local if ring else local,
        mesh=mesh,
        in_specs=placed,
        out_specs=P(("groups", "expert", "sub"), None),
        check_vma=False,
    )
```

```python
import functools

import jax
import jax.numpy as jnp
from jax import lax
from jax.experimental import pallas as pl
from jax.experimental.pallas import tpu as pltpu
from jax.sharding import PartitionSpec as P

RING = 8
PARTS = 2
FF_TILE = 256
D_TILE = 512


def local(tokens, router_probs, expert_ids, slot_expert, w_gate, w_up, w_down):
    tok_rows, width = tokens.shape
    top = expert_ids.shape[1]
    experts = slot_expert.shape[0]
    capacity = min(tok_rows, max(2, (tok_rows * top + experts - 1) // experts))
    gates = router_probs / jnp.sum(router_probs, axis=1, keepdims=True)
    flat_ids = expert_ids.reshape(-1)
    numbers = jnp.arange(experts, dtype=jnp.int32)
    slot_of = jnp.sum(
        jnp.where(slot_expert[None, :] == flat_ids[:, None], numbers[None, :], 0), axis=1
    )
    hits = (flat_ids[:, None] == numbers[None, :]).astype(jnp.int32)
    before = jnp.cumsum(hits, axis=0) - hits
    rank = jnp.sum(before * hits, axis=1)
    target = slot_of * capacity + rank
    select = (target[:, None] == jnp.arange(experts * capacity, dtype=jnp.int32)[None, :]).astype(
        jnp.float32
    )
    select = select.reshape(tok_rows, top, experts * capacity)
    spread = jnp.sum(select, axis=1).astype(jnp.bfloat16)
    weights_mix = jnp.einsum("tk,tkr->tr", gates, select)
    outgoing = jnp.einsum("tr,td->rd", spread, tokens, preferred_element_type=jnp.float32).astype(
        jnp.bfloat16
    )
    outgoing = outgoing.reshape(experts, capacity, width)
    arrived = lax.all_to_all(outgoing, "expert", split_axis=0, concat_axis=0, tiled=True)
    both = lax.all_gather(arrived, "sub", axis=0, tiled=True).reshape(-1, width)
    gate_in = jnp.dot(both, w_gate[0], preferred_element_type=jnp.float32)
    up_in = jnp.dot(both, w_up[0], preferred_element_type=jnp.float32)
    hidden = (jax.nn.silu(gate_in) * up_in).astype(jnp.bfloat16)
    summed = lax.psum_scatter(
        jnp.dot(hidden, w_down[0], preferred_element_type=jnp.float32).astype(jnp.bfloat16),
        "sub",
        scatter_dimension=0,
        tiled=True,
    )
    returned = lax.all_to_all(
        summed.reshape(experts, capacity, width), "expert", split_axis=0, concat_axis=0, tiled=True
    )
    outputs = returned.reshape(experts * capacity, width)
    weight_high = weights_mix.astype(jnp.bfloat16)
    weight_low = (weights_mix - weight_high.astype(jnp.float32)).astype(jnp.bfloat16)
    mixed = jnp.dot(weight_high, outputs, preferred_element_type=jnp.float32)
    mixed = mixed + jnp.dot(weight_low, outputs, preferred_element_type=jnp.float32)
    return mixed.astype(jnp.bfloat16)


def ring_place(e):
    z, x, core = lax.div(e, 4), lax.rem(lax.div(e, 2), 2), lax.rem(e, 2)
    return x * (RING - 1 - z) + (1 - x) * z, core


def ring_index(place, core):
    x = lax.div(place, RING // 2)
    z = x * (RING - 1 - place) + (1 - x) * place
    return z * 4 + x * 2 + core


def long_slot(s):
    return 2 * s - 1 if s else 0


def short_slot(s):
    return 2 * s


def other_slot(slot):
    if slot in (0, RING - 1):
        return slot
    return slot + 1 if slot % 2 else slot - 1


def kernel(
    tokens, probs_in, ids_in, slots_in, w_gate, w_up, w_down, out, last_in,
    probs, ids, slots, x, mix, vg, vu, vd, hidden, own, away, near, long_out, long_in, short_out, short_in,
    in_sem, w_sem, ag_send, ag_recv, sib_send, sib_recv, near_send, near_recv,
    long_send, long_recv, short_send, short_recv,
    rest, out_sem,
):
    rows, width = tokens.shape
    half = rows // PARTS
    ff = hidden.shape[1]
    me = lax.axis_index("expert")
    place, core = ring_place(me)
    step = 1 - 2 * core
    ahead = ring_index(lax.rem(place + step + RING, RING), core)
    behind = ring_index(lax.rem(place - step + RING, RING), core)
    sibling = me + step

    def device(e):
        return (lax.axis_index("groups"), e, lax.axis_index("sub"))

    def remote(src, dst, send, recv, e):
        return pltpu.make_async_remote_copy(
            src_ref=src, dst_ref=dst, send_sem=send, recv_sem=recv,
            device_id=device(e), device_id_type=pl.DeviceIdType.MESH,
        )

    barrier = pltpu.get_barrier_semaphore()
    for e in (ahead, behind, sibling):
        pl.semaphore_signal(barrier, inc=1, device_id=device(e), device_id_type=pl.DeviceIdType.MESH)

    smalls = [
        pltpu.make_async_copy(probs_in, probs, in_sem.at[0]),
        pltpu.make_async_copy(ids_in, ids, in_sem.at[1]),
        pltpu.make_async_copy(slots_in, slots, in_sem.at[2]),
    ]
    loads = [
        pltpu.make_async_copy(tokens, x.at[pl.ds(0, rows), :], w_sem.at[0]),
        pltpu.make_async_copy(w_gate.at[0], vg, w_sem.at[1]),
        pltpu.make_async_copy(w_up.at[0], vu, w_sem.at[2]),
        pltpu.make_async_copy(w_down.at[0], vd, w_sem.at[3]),
    ]
    for load in smalls:
        load.start()

    pl.semaphore_wait(barrier, 3)

    def view(slot, side, part):
        if part == PARTS:
            return mix.at[slot, side]
        return x.at[pl.ds(slot * 2 * rows + side * rows + part * half, half), :]

    def held_at(slot, part):
        if slot == 0 and part < PARTS:
            return tokens.at[pl.ds(part * half, half), :]
        return view(slot, 0, part)

    sends, stores = [], []

    def ring_copy(src, dst, part, e):
        return remote(held_at(src, part), view(dst, 0, part), ag_send.at[dst, part], ag_recv.at[dst, part], e)

    def sib_copy(slot, part):
        dst = other_slot(slot)
        return remote(held_at(slot, part), view(dst, 1, part), sib_send.at[dst, part], sib_recv.at[dst, part], sibling)

    def start(copy):
        copy.start()
        sends.append(copy)

    for part in range(PARTS):
        start(ring_copy(0, long_slot(1), part, ahead))
        start(ring_copy(0, short_slot(1), part, behind))
    for part in range(PARTS):
        start(sib_copy(0, part))
    for load in loads:
        load.start()
    for load in smalls:
        load.wait()

    p = probs[...]
    gates = p / jnp.sum(p, axis=0, keepdims=True)
    experts = mix.shape[2]
    number = lax.broadcasted_iota(jnp.int32, (experts, rows), 0)
    held = jnp.zeros((experts, rows), jnp.int32)
    for j in range(experts):
        held = jnp.where(number == j, slots[j], held)
    weight = jnp.zeros((experts, rows), jnp.float32)
    for k in range(p.shape[0]):
        weight = weight + jnp.where(ids[k:k + 1, :] == held, gates[k:k + 1, :], 0.0)
    mix[0, 0, :, 0:rows] = weight
    mix[0, 0, :, rows:] = jnp.zeros((experts, mix.shape[3] - rows), jnp.float32)
    start(ring_copy(0, long_slot(1), PARTS, ahead))
    start(ring_copy(0, short_slot(1), PARTS, behind))
    start(sib_copy(0, PARTS))

    def await_sib(slot, part):
        remote(held_at(other_slot(slot), part), view(slot, 1, part), sib_send.at[slot, part], sib_recv.at[slot, part], sibling).wait_recv()

    def arrive(s, parts):
        for part in parts:
            ring_copy(long_slot(s - 1), long_slot(s), part, ahead).wait_recv()
            if s < RING // 2:
                start(ring_copy(long_slot(s), long_slot(s + 1), part, ahead))
            else:
                start(sib_copy(long_slot(s), part))
            if s < RING // 2:
                ring_copy(short_slot(s - 1), short_slot(s), part, behind).wait_recv()
                if s < RING // 2 - 1:
                    start(ring_copy(short_slot(s), short_slot(s + 1), part, behind))
                start(sib_copy(long_slot(s), part))
                start(sib_copy(short_slot(s), part))

    def first_items(group):
        base, count = group[0] * 2 * rows, len(group) * 2 * rows

        def ready():
            for slot in group:
                for part in range(PARTS):
                    await_sib(slot, part)

        def tile(j):
            if j == 0:
                ready()
            cols = pl.ds(j * FF_TILE, FF_TILE)
            a = x[base:base + count, :]
            g = jnp.dot(a, vg[:, cols], preferred_element_type=jnp.float32)
            u = jnp.dot(a, vu[:, cols], preferred_element_type=jnp.float32)
            hidden[0:count, cols] = (g / (1.0 + jnp.exp(-g)) * u).astype(jnp.bfloat16)

        return [functools.partial(tile, j) for j in range(ff // FF_TILE)]

    def column(slot, side):
        table = mix[slot, side]
        row = lax.broadcasted_iota(jnp.int32, table.shape, 0)
        line = jnp.sum(jnp.where(row == me, table, 0.0), axis=0, keepdims=True)
        shape = (rows, table.shape[1])
        same = lax.broadcasted_iota(jnp.int32, shape, 0) == lax.broadcasted_iota(jnp.int32, shape, 1)
        return jnp.sum(jnp.where(same, line, 0.0), axis=1, keepdims=True)

    def near_copy(slot):
        dst = other_slot(slot)
        return remote(away.at[slot], near.at[dst], near_send.at[dst], near_recv.at[dst], sibling)

    def second_items(group):
        count = len(group) * 2 * rows
        scale = []

        def tile(j):
            if j == 0:
                for slot in group:
                    await_sib(slot, PARTS)
                scale.append(jnp.concatenate([column(slot, side) for slot in group for side in (0, 1)], axis=0))
            cols = pl.ds(j * D_TILE, D_TILE)
            y = jnp.dot(hidden[0:count, :], vd[:, cols], preferred_element_type=jnp.float32)
            y = y.astype(jnp.bfloat16).astype(jnp.float32) * scale[0]
            for i, slot in enumerate(group):
                own[slot, :, cols] = y[2 * i * rows:(2 * i + 1) * rows]
                away[slot, :, cols] = y[(2 * i + 1) * rows:(2 * i + 2) * rows].astype(jnp.bfloat16)
            if j == width // D_TILE - 1:
                for slot in group:
                    start(near_copy(slot))

        return [functools.partial(tile, j) for j in range(width // D_TILE)]

    def await_near(slot):
        remote(away.at[other_slot(slot)], near.at[slot], near_send.at[slot], near_recv.at[slot], sibling).wait_recv()

    groups = [[0]] + [[long_slot(s), short_slot(s)] for s in range(1, RING // 2)] + [[RING - 1]]

    for s in range(1, RING // 2 + 1):
        items = first_items(groups[s - 1]) + second_items(groups[s - 1])
        for part in range(PARTS):
            arrive(s, (part,) if part else (part, PARTS))
            if s == 1 and part == 0:
                for load in loads:
                    load.wait()
            for item in items[len(items) * part // PARTS:len(items) * (part + 1) // PARTS]:
                item()

    def pass_on(k, far, slot_at, out_ref, in_ref, send, recv, e):
        slot = slot_at(far - k)
        if k == 0:
            await_near(slot)
        elif far - k:
            await_near(slot)
        for h in range(PARTS):
            at = pl.ds(h * half, half)
            if k:
                remote(out_ref.at[k - 1, at, :], in_ref.at[k - 1, at, :], send.at[k - 1, h], recv.at[k - 1, h], e).wait_recv()
            total = own[slot, at, :] + near[slot, at, :].astype(jnp.float32)
            if k:
                total = total + in_ref[k - 1, at, :].astype(jnp.float32)
            out_ref[k, at, :] = total.astype(jnp.bfloat16)
            landing = last_in.at[at, :] if k == RING // 2 - 1 else in_ref.at[k, at, :]
            start(remote(out_ref.at[k, at, :], landing, send.at[k, h], recv.at[k, h], e))

    def pass_long(k):
        pass_on(k, RING // 2, long_slot, long_out, long_in, long_send, long_recv, behind)

    def pass_short(k):
        pass_on(k, RING // 2 - 1, short_slot, short_out, short_in, short_send, short_recv, ahead)

    for item in first_items(groups[-1]):
        item()
    pass_short(0)
    for item in second_items(groups[-1]):
        item()
    pass_long(0)
    for k in range(1, RING // 2 - 1):
        pass_short(k)
        pass_long(k)
    pass_long(RING // 2 - 1)

    await_near(0)
    last = RING // 2 - 1
    for h in range(PARTS):
        at = pl.ds(h * half, half)
        remote(short_out.at[last - 1, at, :], short_in.at[last - 1, at, :], short_send.at[last - 1, h], short_recv.at[last - 1, h], ahead).wait_recv()
        total = own[0, at, :] + near[0, at, :].astype(jnp.float32)
        rest[at, :] = total + short_in[last - 1, at, :].astype(jnp.float32)
        store = pltpu.make_async_copy(rest.at[at, :], out.at[at, :], out_sem.at[h])
        store.start()
        stores.append(store)
    for h in range(PARTS):
        at = pl.ds(h * half, half)
        remote(long_out.at[last, at, :], last_in.at[at, :], long_send.at[last, h], long_recv.at[last, h], behind).wait_recv()
    for store in stores:
        store.wait()
    for copy in sends:
        copy.wait_send()


def ring_local(tokens, router_probs, expert_ids, slot_expert, w_gate, w_up, w_down):
    rows, width = tokens.shape
    ff = w_gate.shape[2]
    experts = slot_expert.shape[0]
    hops = RING // 2
    bf16, f32 = jnp.bfloat16, jnp.float32
    dma = pltpu.SemaphoreType.DMA
    hbm = pl.BlockSpec(memory_space=pl.ANY)
    here, arrived = pl.pallas_call(
        kernel,
        out_shape=(jax.ShapeDtypeStruct((rows, width), f32), jax.ShapeDtypeStruct((rows, width), bf16)),
        in_specs=[hbm] * 7,
        out_specs=(hbm, hbm),
        scratch_shapes=[
            pltpu.VMEM(router_probs.shape[::-1], f32),
            pltpu.VMEM(expert_ids.shape[::-1], jnp.int32),
            pltpu.SMEM(slot_expert.shape, jnp.int32),
            pltpu.VMEM((RING * 2 * rows, width), bf16),
            pltpu.VMEM((RING, 2, experts, 128), f32),
            pltpu.VMEM((width, ff), bf16),
            pltpu.VMEM((width, ff), bf16),
            pltpu.VMEM((ff, width), bf16),
            pltpu.VMEM((4 * rows, ff), bf16),
            pltpu.VMEM((RING, rows, width), f32),
            pltpu.VMEM((RING, rows, width), bf16),
            pltpu.VMEM((RING, rows, width), bf16),
            pltpu.VMEM((hops, rows, width), bf16),
            pltpu.VMEM((hops - 1, rows, width), bf16),
            pltpu.VMEM((hops - 1, rows, width), bf16),
            pltpu.VMEM((hops - 1, rows, width), bf16),
            dma((3,)), dma((4,)),
            dma((RING, PARTS + 1)), dma((RING, PARTS + 1)), dma((RING, PARTS + 1)), dma((RING, PARTS + 1)),
            dma((RING,)), dma((RING,)),
            dma((hops, PARTS)), dma((hops, PARTS)), dma((hops - 1, PARTS)), dma((hops - 1, PARTS)),
            pltpu.VMEM((rows, width), f32), dma((PARTS,)),
        ],
        compiler_params=pltpu.CompilerParams(
            collective_id=0, has_side_effects=True, vmem_limit_bytes=60 * 2**20
        ),
        cost_estimate=pl.CostEstimate(
            flops=6 * RING * 2 * rows * width * ff, bytes_accessed=6 * width * ff, transcendentals=0
        ),
    )(tokens, router_probs.T, expert_ids.T, slot_expert, w_gate, w_up, w_down)
    return (here + arrived.astype(f32)).astype(bf16)


def solution(mesh):
    placed = (
        P(("groups", "expert", "sub"), None),
        P(("groups", "expert", "sub"), None),
        P(("groups", "expert", "sub"), None),
        P(),
        P("expert", None, "sub"),
        P("expert", None, "sub"),
        P("expert", "sub", None),
    )
    ring = mesh.shape["sub"] == 1 and mesh.shape["expert"] == 2 * RING
    return jax.shard_map(
        ring_local if ring else local,
        mesh=mesh,
        in_specs=placed,
        out_specs=P(("groups", "expert", "sub"), None),
        check_vma=False,
    )
```
